128 devices in a mesh: dp: 16 (over z, x_lo, core), mp: 8 (over y, x_hi).
Axes of the slice: x: 4 (x_hi: 2, x_lo: 2; x = x_hi * 2 + x_lo), y: 4, z: 4, core: 2. Of those that a mesh axis runs over, the one named last changes fastest.
Arguments:
- tokens: bfloat16 [16384, 2048], P(('dp', 'mp')), may hold values from -24 to 24
- cotangent: bfloat16 [16384, 2048], P(('dp', 'mp')), may hold values from -24 to 24
- seq_lengths: int32 [16, 4], P('dp'), may hold values from 0 to 1024, as said below
- w_qkv: bfloat16 [2048, 3, 2048], P('dp', None, 'mp'), may hold values from -0.125 to 0.125
- b_qkv: float32 [3, 2048], P(None, 'mp'), may hold values from -1.75 to 1.75
- w_out: bfloat16 [2048, 2048], P('mp', 'dp'), may hold values from -0.75 to 0.75
- b_out: float32 [2048], replicated, may hold values from -1.75 to 1.75
- w_fc1: bfloat16 [2048, 8192], P('dp', 'mp'), may hold values from -0.125 to 0.125
- b_fc1: float32 [8192], P('mp'), may hold values from -3 to 3
- w_fc2: bfloat16 [8192, 2048], P('mp', 'dp'), may hold values from -0.0625 to 0.0625
- b_fc2: float32 [2048], replicated, may hold values from -1.75 to 1.75
- ln_gain: float32 [2048], replicated, may hold values from 0.1 to 1.9
- ln_bias: float32 [2048], replicated, may hold values from -1.75 to 1.75
Outputs:
- mixed: bfloat16 [16384, 2048], P(('dp', 'mp'))
- tokens_grad: bfloat16 [16384, 2048], P(('dp', 'mp'))
- w_qkv_grad: float32 [2048, 3, 2048], P('dp', None, 'mp')
- b_qkv_grad: float32 [3, 2048], P(None, 'mp')
- w_out_grad: float32 [2048, 2048], P('mp', 'dp')
- b_out_grad: float32 [2048], replicated
- w_fc1_grad: float32 [2048, 8192], P('dp', 'mp')
- b_fc1_grad: float32 [8192], P('mp')
- w_fc2_grad: float32 [8192, 2048], P('mp', 'dp')
- b_fc2_grad: float32 [2048], replicated
- ln_gain_grad: float32 [2048], replicated
- ln_bias_grad: float32 [2048], replicated
The draws below stay inside these ranges and needn't reach their ends.
Inputs may be any that keep to these rules, and one draw needn't show every extreme that they name: `seq_lengths`: the four lengths of a data group add up to 1024; a length may be 0. The second sequence starts within the group's first 128 rows and ends within its last 128; in some group it holds all 1024 rows.
All inputs are finite; a program needn't handle non-finite values.
Results may differ from the reference program's by a relative error of at most 0.018.
Values may be sent and summed in bfloat16 or wider, within the bound.
A program may use at most 128 MiB of HBM per device.

```python
import jax
import jax.numpy as jnp
from jax import lax

D = 2048
H = 32
HD = 64
ROT = 32
FF = 8192
GROUP = 1024
ROWS = 128
TOKENS = 16384
N_DP = 16


def draw_seq_lengths(key, part):
    key = jax.random.fold_in(key, 11)
    keys_split = jax.random.split(key, 4)
    first_len = jax.random.randint(keys_split[0], (N_DP,), 0, ROWS)
    second_end = jax.random.randint(keys_split[1], (N_DP,), GROUP - ROWS + 1, GROUP + 1)
    chosen = jax.random.randint(keys_split[2], (), 0, N_DP)
    groups = jnp.arange(N_DP, dtype=jnp.int32)
    first_len = jnp.where(groups == chosen, 0, first_len)
    second_end = jnp.where(groups == chosen, GROUP, second_end)
    third_len = jax.random.randint(keys_split[3], (N_DP,), 0, GROUP - second_end + 1)
    fourth_len = GROUP - second_end - third_len
    return jnp.stack([first_len, second_end - first_len, third_len, fourth_len], axis=1).astype(jnp.int32)


def spiked(entries, own_key, source, target, parts, factor):
    owner, partner = [(jnp.arange(entries.shape[position]) // (entries.shape[position] // parts)).reshape([-1 if axis == position else 1 for axis in range(entries.ndim)]) for position in (source, target)]
    chosen = jax.random.permutation(own_key, parts)[partner]
    strong = (owner == chosen) | (owner == (partner + parts // 2) % parts)
    return jnp.where(strong, factor * entries, entries)


def levels(own_key, extent, cuts, low, top_value):
    def one(dim, parts):
        heights = jax.random.uniform(jax.random.fold_in(jax.random.fold_in(own_key, 6), dim), (parts,), jnp.float32, low / len(cuts), top_value / len(cuts))
        return jnp.repeat(jnp.exp(heights), extent[dim] // parts).reshape((-1,) + (1,) * (len(extent) - dim - 1))

    loudness = one(*cuts[0])
    for cut in cuts[1:]:
        loudness = loudness * one(*cut)
    return loudness


def bell_draw(stream_key, shape, width, most, cuts=(), kind=jnp.bfloat16):
    drawn = jax.random.normal(stream_key, shape, jnp.float32) * width
    if len(cuts) > 0:
        drawn = levels(stream_key, shape, cuts, -0.22, 0.18) * drawn
    return jnp.clip(drawn, min=-most, max=most).astype(kind)


def heavy_noise(stream_key, dims, deviation, most, shards, heavy, kind=jnp.bfloat16):
    values = deviation * jax.random.normal(stream_key, dims, jnp.float32)
    if shards:
        values = values * levels(stream_key, dims, shards, -0.22, 0.18)
    return jnp.clip(spiked(values, jax.random.fold_in(stream_key, 3), *heavy), -most, most).astype(kind)


def setup_inputs(seed: int = 0) -> dict:
    splits = jax.random.split(jax.random.key(seed), 14)
    return {
        "tokens": heavy_noise(splits[0], (TOKENS, D), 1.0, 24.0, ((0, 128),), (0, 1, 128, 5.5)),
        "cotangent": heavy_noise(splits[1], (TOKENS, D), 1.0, 24.0, ((0, 128),), (0, 1, 128, 5.5)),
        "seq_lengths": draw_seq_lengths(jax.random.fold_in(splits[13], 71), 0),
        "w_qkv": bell_draw(splits[3], (D, 3, D), D ** -0.5, 0.125, ((0, 16), (2, 8))),
        "b_qkv": bell_draw(splits[4], (3, D), 0.3, 1.75, ((1, 8),), jnp.float32),
        "w_out": bell_draw(splits[5], (D, D), (D // 32) ** -0.5, 0.75, ((0, 8), (1, 16))),
        "b_out": bell_draw(splits[6], (D,), 0.3, 1.75, (), jnp.float32),
        "w_fc1": bell_draw(splits[7], (D, FF), D ** -0.5, 0.125, ((0, 16), (1, 8))),
        "b_fc1": bell_draw(splits[8], (FF,), 0.5, 3.0, ((0, 8),), jnp.float32),
        "w_fc2": bell_draw(splits[9], (FF, D), FF ** -0.5, 0.0625, ((0, 8), (1, 16))),
        "b_fc2": bell_draw(splits[10], (D,), 0.3, 1.75, (), jnp.float32),
        "ln_gain": jnp.clip(1.0 + 0.18 * jax.random.normal(splits[11], (D,), jnp.float32), 0.1, 1.9),
        "ln_bias": bell_draw(splits[12], (D,), 0.3, 1.75, (), jnp.float32),
    }


@jax.custom_vjp
def low(v):
    return lax.optimization_barrier(v.astype(jnp.bfloat16)).astype(jnp.float32)

@jax.custom_vjp
def low_back(v):
    return v

def low_keep(v):
    return (low(v), None)

def low_pass(kept, grad):
    return (grad,)

def back_keep(v):
    return (v, None)

def back_low(kept, grad):
    return (low(grad),)
low.defvjp(low_keep, low_pass)
low_back.defvjp(back_keep, back_low)
highest = lax.Precision.HIGHEST

def normalize(values, gain_vec, shift_vec):
    center = values - lax.optimization_barrier(jnp.mean(values, axis=-1, keepdims=True))
    spread = lax.optimization_barrier(jnp.mean(center * center, axis=-1, keepdims=True))
    return center * lax.rsqrt(spread + 1e-05) * gain_vec + shift_vec

def rotary(heads, places):
    half_rot = ROT // 2
    freqs = 10000.0 ** (-2.0 * jnp.arange(half_rot, dtype=jnp.float32) / ROT)
    angles = places[:, None] * freqs[None, :]
    cosine = jnp.cos(angles)[:, None, :]
    sine = jnp.sin(angles)[:, None, :]
    first_half = heads[..., :half_rot]
    second_half = heads[..., half_rot:ROT]
    return jnp.concatenate([first_half * cosine - second_half * sine, second_half * cosine + first_half * sine, heads[..., ROT:]], axis=-1)

def layout(lengths, total_rows):
    ends = jnp.cumsum(lengths).astype(jnp.int32)
    starts = (ends - lengths).astype(jnp.int32)
    row_ids = jnp.arange(total_rows, dtype=jnp.int32)
    segment = lax.optimization_barrier(jnp.sum((row_ids[:, None] >= ends[None, :3]).astype(jnp.int32), axis=1)).astype(jnp.int32)
    slots = jnp.arange(4, dtype=jnp.int32)
    begin = lax.optimization_barrier(jnp.sum(jnp.where(segment[:, None] == slots[None, :], starts[None, :], 0), axis=1)).astype(jnp.int32)
    return (row_ids, segment, row_ids - begin)

def group_forward(values, params, row_ids, segment, places):
    w_qkv, b_qkv, w_out, b_out, w_fc1, b_fc1, w_fc2, b_fc2, ln_gain, ln_bias = params
    total_rows = values.shape[0]
    normed = low(normalize(values, ln_gain, ln_bias))
    mixed_qkv = low_back(jnp.einsum('gd,dte->gte', normed, w_qkv, precision=highest) + b_qkv[None])
    shaped = mixed_qkv.reshape(total_rows, 3, H, HD)
    angle_pos = places.astype(jnp.float32)
    queries = low(rotary(shaped[:, 0], angle_pos))
    keys_rot = low(rotary(shaped[:, 1], angle_pos))
    values_h = low(shaped[:, 2])
    allowed = (segment[:, None] == segment[None, :]) & (row_ids[None, :] <= row_ids[:, None])

    def one_head(operands):
        query_h, key_h, value_h = operands
        scores = low_back(jnp.dot(query_h, key_h.T, precision=highest) * HD ** (-0.5))
        scores = jnp.where(allowed, scores, -1e+30)
        peak = lax.optimization_barrier(jnp.max(scores, axis=-1, keepdims=True))
        expo = jnp.exp(scores - peak)
        probs = expo / lax.optimization_barrier(jnp.sum(expo, axis=-1, keepdims=True))
        return jnp.dot(low(probs), value_h, precision=highest)
    heads_out = lax.map(jax.checkpoint(one_head), (jnp.swapaxes(queries, 0, 1), jnp.swapaxes(keys_rot, 0, 1), jnp.swapaxes(values_h, 0, 1)))
    attended = low(low_back(jnp.swapaxes(heads_out, 0, 1).reshape(total_rows, D)))
    branch_attn = jnp.dot(attended, w_out, precision=highest) + b_out
    hidden_pre = low_back(jnp.dot(normed, w_fc1, precision=highest) + b_fc1)
    branch_mlp = jnp.dot(low(jax.nn.gelu(hidden_pre, approximate=True)), w_fc2, precision=highest) + b_fc2
    return values + low_back(branch_attn + branch_mlp)

def reference(tokens, cotangent, seq_lengths, w_qkv, b_qkv, w_out, b_out, w_fc1, b_fc1, w_fc2, b_fc2, ln_gain, ln_bias):
    params = tuple((item.astype(jnp.float32) for item in (w_qkv, b_qkv, w_out, b_out, w_fc1, b_fc1, w_fc2, b_fc2, ln_gain, ln_bias)))
    input_groups = tokens.astype(jnp.float32).reshape(N_DP, GROUP, D)
    grad_groups = cotangent.astype(jnp.float32).reshape(N_DP, GROUP, D)

    def one_group(totals, operands):
        group_in, group_grad, lengths = operands
        row_ids, segment, places = layout(lengths, GROUP)
        result, backward = jax.vjp(lambda values, weights: group_forward(values, weights, row_ids, segment, places), group_in, params)
        input_grad, param_grads = backward(group_grad)
        summed = tuple((left + right for left, right in zip(totals, param_grads)))
        return (summed, (result.astype(jnp.bfloat16), input_grad.astype(jnp.bfloat16)))
    initial = tuple((jnp.zeros_like(item) for item in params))
    totals, (outputs, input_grads) = lax.scan(one_group, initial, (input_groups, grad_groups, seq_lengths))
    return (outputs.reshape(TOKENS, D), input_grads.reshape(TOKENS, D), totals[0], totals[1], totals[2], totals[3], totals[4], totals[5], totals[6], totals[7], totals[8], totals[9])
```

```python
import jax
import jax.numpy as jnp
import numpy as np
from jax import lax
from jax.experimental import pallas as pl
from jax.experimental.pallas import tpu as pltpu
from jax.sharding import PartitionSpec as P

HD = 64
ROT = 32
MESH = pl.DeviceIdType.MESH
BF16 = jnp.bfloat16
F32 = jnp.float32
ROWS = 128
GROUP = 1024
D = 2048
QKV = 768
FC = 1024
IN_W = QKV + FC
OUT_W = 256 + FC
ALL_W = IN_W + OUT_W
LOG2E = 1.4426950408889634
LN2 = 0.6931471805599453
CHUNKS = 4
CHUNK = D // CHUNKS
KEEP = 96
VMEM_LIMIT = 64 * 1024 * 1024 - 65536

ORDER = (
    "Wi.go", "ln", "X.go", "X.x", "wprep", "tab", "Wi.f1", "X.f1", "Wi.p", "Wi.c1", "Y.x", "X.p", "X.q1", "X.q2",
    "Wi.f2", "Wi.c2", "Wo.go", "Wo.x", "X.f2", "Y.go", "Wi.c3", "Wo.f1", "proj", "Y.f1", "Y.q1", "Y.p", "Wo.p",
    "Wo.c1", "attf", "Wo.f2", "Wo.c2", "Y.q2", "Wo.c3", "Y.f2", "p1", "r10_qa", "backs", "r10_s1b", "r11_qa",
    "r11_s1b", "r12_qa", "r13_qa", "dwo0", "r10_s1a", "dwo1", "dwo2", "ko.t0", "dwo3", "ko.t1", "attb0", "r10_th",
    "r11_s1a", "r12_s1a", "r12_s1b", "ko.t2", "ko.t3", "ro.s1b", "attb1", "r11_th", "r12_th", "r13_s1a", "r13_s1b",
    "ro.s1a", "bias", "p2.0", "p2.1", "r13_th", "p2.2", "r20_s1b", "ro.th", "p2.3", "r20_qa", "r21_s1b", "pool",
    "dwi0", "dwi1", "mix", "r20_s1a", "r21_qa", "kq.t0", "dwi2", "r22_qa", "kf.t0", "kf.t1", "r23_qa", "kq.t1",
    "dwi3", "kq.t2", "kf.t2", "rq.s1b", "rq.s1a", "r20_th", "r22_s1b", "r21_s1a", "kq.t3", "kf.t3", "r22_s1a",
    "r21_th", "r23_s1a", "r23_s1b", "r22_th", "rf.s1b", "r23_th", "rf.s1a", "sums", "rq.th", "lasto", "back",
    "sum_x", "sum_z", "lastq", "rf.th", "sum_y", "lastf",
)

VMEM = pl.BlockSpec(memory_space=pltpu.VMEM)
ANY = pl.BlockSpec(memory_space=pl.ANY)


def place():
    dp = lax.axis_index("dp")
    mp = lax.axis_index("mp")
    return dp, mp


def peers():
    dp, mp = place()
    z, low = dp // 4, dp % 4
    y, xh = mp // 2, mp % 2
    core = low % 2
    xl = low // 2
    flipped = z * 4 + (1 - xl) * 2 + core
    return {
        "core": (z * 4 + xl * 2 + (1 - core), mp),
        "xp": (flipped, y * 2 + (xh + xl) % 2),
        "xm": (flipped, y * 2 + (xh + 1 - xl) % 2),
        "xx": (dp, y * 2 + (1 - xh)),
        "xl": (flipped, mp),
        "xp2": (flipped + 1 - 2 * core, y * 2 + (xh + xl) % 2),
        "xm2": (flipped + 1 - 2 * core, y * 2 + (xh + 1 - xl) % 2),
        "xx2": (dp + 1 - 2 * core, y * 2 + (1 - xh)),
        "zp": (((z + 1) % 4) * 4 + low, mp),
        "zm": (((z + 3) % 4) * 4 + low, mp),
        "zz": (((z + 2) % 4) * 4 + low, mp),
        "yp": (dp, ((y + 1) % 4) * 2 + xh),
        "ym": (dp, ((y + 3) % 4) * 2 + xh),
        "yy": (dp, ((y + 2) % 4) * 2 + xh),
    }


class remote:
    def __init__(self, src, dst, send, recv, target):
        self.parts = dict(
            src_ref=src, dst_ref=dst, send_sem=send, recv_sem=recv, device_id=target, device_id_type=MESH
        )

    def start(self):
        pltpu.make_async_remote_copy(**self.parts).start()

    def wait(self):
        pltpu.make_async_remote_copy(**self.parts).wait()

    def wait_send(self):
        pltpu.make_async_remote_copy(**self.parts).wait_send()

    def wait_recv(self):
        pltpu.make_async_remote_copy(**self.parts).wait_recv()


def rows_at(start, count):
    return pl.ds(pl.multiple_of(start, 16), count)


def mp_slots():
    _, mp = place()
    y, xh = mp // 2, mp % 2

    def at(step):
        base = ((y + step) % 4) * 2
        return (base + xh, base + (1 - xh))

    return mp, at(0)[1], at(1), at(3), at(2)


def dp_slots():
    dp, _ = place()
    z, xl, core = dp // 4, (dp // 2) % 2, dp % 2

    def at(step):
        base = ((z + step) % 4) * 4 + core
        return (base + xl * 2, base + (1 - xl) * 2)

    return dp, at(0)[1], at(1), at(3), at(2)


class RingGather:
    def __init__(self, piece, slots, pair, up, down, send, recv, keep=ROWS):
        slot, pair_slot, plus, minus, opposite = slots
        half, mid = ROWS // 2, keep // 2

        def copy(index, which, target, start=0, count=ROWS):
            part = piece(which, start, count)
            return remote(part, part, send.at[index], recv.at[index], target)

        self.go = [
            copy(0, slot, pair),
            copy(1, slot, up),
            copy(2, slot, down),
            copy(3, pair_slot, up, 0, keep),
            copy(4, pair_slot, down, 0, keep),
            copy(5, minus[0], up, 0, half),
            copy(6, plus[0], down, half, half),
            copy(7, minus[1], up, 0, mid),
            copy(8, plus[1], down, mid, mid),
        ]
        self.come = [
            copy(0, pair_slot, pair),
            copy(1, minus[0], up),
            copy(2, plus[0], down),
            copy(3, minus[1], up, 0, keep),
            copy(4, plus[1], down, 0, keep),
            copy(5, opposite[0], up, 0, half),
            copy(6, opposite[0], down, half, half),
            copy(7, opposite[1], up, 0, mid),
            copy(8, opposite[1], down, mid, mid),
        ]
        if keep < ROWS:
            for index, two in ((9, minus), (10, plus), (11, opposite)):
                self.go.append(copy(index, two[0], pair, keep, ROWS - keep))
                self.come.append(copy(index, two[1], pair, keep, ROWS - keep))

    def start(self, *which):
        for i in which:
            self.go[i].start()

    def arrived(self, *which):
        for i in which:
            self.come[i].wait_recv()

    def sent(self):
        for c in self.go:
            c.wait_send()


class CoreShare:
    def __init__(self, ref, target, send, recv):
        slot, pair_slot, plus, minus, opposite = dp_slots()
        half = ROWS // 2
        flip = 1 - 2 * (place()[0] % 2)
        pieces = [
            (pair_slot, 0, ROWS),
            (minus[0], 0, ROWS),
            (plus[0], 0, ROWS),
            (minus[1], 0, ROWS),
            (plus[1], 0, ROWS),
            (opposite[0], 0, half),
            (opposite[0], half, half),
            (opposite[1], 0, half),
            (opposite[1], half, half),
            (slot, 0, ROWS),
        ]

        def copy(index, which, start, count):
            piece = ref.at[rows_at(which * ROWS + start, count)]
            return remote(piece, piece, send.at[index], recv.at[index], target)

        self.go = [copy(i, s, a, n) for i, (s, a, n) in enumerate(pieces)]
        self.come = [copy(i, s + flip, a, n) for i, (s, a, n) in enumerate(pieces)]

    def start(self, *which):
        for i in which:
            self.go[i].start()

    def arrived(self):
        for c in self.come:
            c.wait_recv()

    def sent(self):
        for c in self.go:
            c.wait_send()


def each(count, body, size=16, start=0):
    def step(i, carry):
        body(pl.ds(pl.multiple_of(i * size, size), size))
        return carry

    lax.fori_loop(start // size, count // size, step, 0)


def add_into(dst, term):
    def body(at):
        dst[at, :] = dst[at, :] + term[at, :]

    each(dst.shape[0], body, 32)


class RingReduce:
    def __init__(self, part, slots, who, names, half, full, across, send, recv, keep=ROWS, rest=()):
        slot, pair_slot, plus, minus, opposite = slots
        pair, up, down = (who[name] for name in names)
        self.part, self.slot, self.full, self.across = part, slot, full, across
        self.half, self.keep = half, keep
        self.pair_part = part(pair_slot, keep)
        self.plus_own, self.minus_pair = part(plus[0], ROWS), part(minus[1], keep)

        def go(index, src, dst, target):
            return remote(src, dst, send.at[index], recv.at[index], target)

        self.sends = [
            go(0, part(opposite[0], ROWS), half(0, ROWS), up),
            go(1, part(opposite[1], keep), half(1, keep), down),
            go(2, part(plus[1], keep), full(0, 1, keep), up),
            go(3, part(minus[0], ROWS), full(1, 0, ROWS), down),
            go(4, self.plus_own, full(0, 0, ROWS), up),
            go(5, self.minus_pair, full(1, 1, keep), down),
            go(6, self.pair_part, across, pair),
        ]
        if rest:
            rest_of, self.rest, self.rest_at = rest
            self.sends.append(go(7, rest_of, self.rest, pair))

    def start(self, *which):
        for i in which:
            self.sends[i].start()

    def add_rest(self):
        self.sends[7].wait_recv()
        for place_on_ring in range(4):
            add_into(self.rest_at(place_on_ring), self.rest.at[place_on_ring])

    def up_term(self):
        self.sends[0].wait_recv()
        add_into(self.plus_own, self.half(0, ROWS))
        self.start(4)

    def down_term(self):
        self.sends[1].wait_recv()
        add_into(self.minus_pair, self.half(1, self.keep))
        self.start(5)

    def third(self):
        for i in (2, 3, 4, 5):
            self.sends[i].wait_recv()
        dst, a, b = self.pair_part, self.full(0, 1, self.keep), self.full(1, 1, self.keep)

        def body(at):
            total = dst[at, :].astype(F32) + a[at, :].astype(F32) + b[at, :].astype(F32)
            dst[at, :] = total.astype(dst.dtype)

        each(self.keep, body, 32)
        self.start(6)

    def arrived(self):
        self.sends[6].wait_recv()

    def total(self, at):
        return (
            self.part(self.slot, ROWS)[at, :].astype(F32)
            + self.full(0, 0, ROWS)[at, :].astype(F32)
            + self.full(1, 0, ROWS)[at, :].astype(F32)
            + self.across[at, :].astype(F32)
        )

    def sent(self):
        for c in self.sends:
            c.wait_send()


def dot_nn(a, b):
    return jnp.dot(a, b, preferred_element_type=F32)


def dot_nt(a, b):
    return lax.dot_general(a, b, (((1,), (1,)), ((), ())), preferred_element_type=F32)


def dot_tn(a, b):
    return lax.dot_general(a, b, (((0,), (0,)), ((), ())), preferred_element_type=F32)


def block_kernel(
    tokens_in, cot_in, lens, wq, bq, wo_in, bo, wf1, b1, wf2_in, b2, gain, shift, freq, sign,
    mixed_out, tgrad_out, gin_out, gout_out, small_out,
    tokens, cot, wo, wf2, gin, gout, small, into, out_of,
    x, y, win, wout, ah, qp, dout, pool, p1, cos, sin, dk, dv,
    h1, f1, a1, q1, h2, f2, a2, q2, hi, fi, ai, ho, fo, ao, co, got_x, got, kt, vt,
    xs, xr, ys, yr, wis, wir, cis, cir, wos, wor, cos_s, cos_r,
    r1s, r1r, r2s, r2r, rfs, rfr, rqs, rqr, ros, ror, kfs, kfr, kqs, kqr, kos, kor, sms, smr, free,
):
    who = peers()
    dp, mp = place()
    core, xl, xh = dp % 2, (dp // 2) % 2, mp % 2
    z, yy = dp // 4, mp // 2
    barrier = pltpu.get_barrier_semaphore()
    met = [who[n] for n in ("core", "xp", "xm", "xx", "xp2", "xm2", "xx2", "zp", "zm", "zz", "yp", "ym", "yy")]
    for target in met:
        pl.semaphore_signal(barrier, inc=1, device_id=target, device_id_type=MESH)

    wrow = rows_at(dp * ROWS, ROWS)
    brought = [(wq.at[t], win.at[wrow, t * 256 : (t + 1) * 256]) for t in range(3)]
    brought += [(wf1, win.at[wrow, QKV:IN_W]), (tokens_in, tokens), (wo_in, wo), (wf2_in, wf2)]
    brought += [(cot_in, cot), (cot_in, y.at[yy, xh])]
    brought = [pltpu.make_async_copy(src, dst, into.at[i]) for i, (src, dst) in enumerate(brought)]
    for c in brought:
        c.start()

    def bring(*which):
        for i in which:
            brought[i].wait()

    def send_out(index, src, dst):
        pltpu.make_async_copy(src, dst, out_of.at[index]).start()

    mixed, tgrad = p1.at[yy, xh], y.at[yy, xh]
    outputs = ((mixed, mixed_out), (tgrad, tgrad_out), (gin, gin_out), (gout, gout_out), (small, small_out))
    pl.semaphore_wait(barrier, len(met))

    def flat(ref):
        return lambda slot, start, count: ref.at[rows_at(slot * ROWS + start, count)]

    def deep(ref):
        return lambda slot, start, count: ref.at[slot // 2, slot % 2, start : start + count]

    gx = RingGather(flat(x), mp_slots(), who["xx"], who["yp"], who["ym"], xs, xr, KEEP)
    gy = RingGather(deep(y), mp_slots(), who["xx"], who["yp"], who["ym"], ys, yr, KEEP)
    gi = RingGather(flat(win), dp_slots(), who["xl"], who["zp"], who["zm"], wis, wir)
    go = RingGather(flat(wout), dp_slots(), who["xl"], who["zp"], who["zm"], wos, wor)
    ci = CoreShare(win, who["core"], cis, cir)
    co_ = CoreShare(wout, who["core"], cos_s, cos_r)
    steps = {}

    def step(function):
        steps[function.__name__] = function
        return function

    def transfers(name, *actions):
        def act():
            for action, *which in actions:
                action(*which)

        steps[name] = act

    transfers("Wi.go", (bring, 0, 1, 2, 3), (gi.start, 1, 2, 0), (ci.start, 9))
    transfers("Wi.p", (gi.arrived, 0), (gi.start, 3, 4))
    transfers("Wi.f1", (gi.arrived, 1), (gi.start, 5), (gi.arrived, 2), (gi.start, 6))
    transfers("Wi.f2", (gi.arrived, 3), (gi.start, 7), (gi.arrived, 4), (gi.start, 8))
    transfers("Wi.c1", (ci.start, 0, 1, 2))
    transfers("Wi.c2", (ci.start, 3, 4))
    transfers("Wi.c3", (gi.arrived, 5, 6, 7, 8), (ci.start, 5, 6, 7, 8))
    transfers("Wo.go", (go.start, 1, 2), (co_.start, 9))
    transfers("Wo.x", (go.start, 0))
    transfers("Wo.p", (go.arrived, 0), (go.start, 3, 4))
    transfers("Wo.f1", (go.arrived, 1), (go.start, 5), (go.arrived, 2), (go.start, 6))
    transfers("Wo.f2", (go.arrived, 3), (go.start, 7), (go.arrived, 4), (go.start, 8))
    transfers("Wo.c1", (co_.start, 0, 1, 2))
    transfers("Wo.c2", (co_.start, 3, 4))
    transfers("Wo.c3", (go.arrived, 5, 6, 7, 8), (co_.start, 5, 6, 7, 8))
    for name, ring in (("X", gx), ("Y", gy)):
        transfers(f"{name}.p", (ring.arrived, 0), (ring.start, 3, 4))
        transfers(f"{name}.f1", (ring.arrived, 1), (ring.start, 5), (ring.arrived, 2), (ring.start, 6))
        transfers(f"{name}.f2", (ring.arrived, 3), (ring.start, 7), (ring.arrived, 4), (ring.start, 8))
        transfers(f"{name}.q1", (ring.start, 9, 10))
        transfers(f"{name}.q2", (ring.arrived, 6), (ring.start, 11))
    transfers("X.go", (gx.start, 1, 2))
    transfers("X.x", (gx.start, 0))
    transfers("Y.go", (gy.start, 1, 2))
    transfers("Y.x", (gy.start, 0))

    def norm_rows(i, carry):
        at = pl.ds(pl.multiple_of(i * 16, 16), 16)
        values = tokens[at, :].astype(F32)
        center = values - jnp.mean(values, axis=-1, keepdims=True)
        spread = jnp.mean(center * center, axis=-1, keepdims=True)
        normed = center * lax.rsqrt(spread + 1e-05) * gain[...] + shift[...]
        x[rows_at(mp * ROWS + i * 16, 16), :] = normed.astype(BF16)
        return carry

    @step
    def ln():
        bring(4)
        lax.fori_loop(0, ROWS // 16, norm_rows, 0)

    @step
    def wprep():
        bring(5, 6, 7, 8)
        wout[wrow, 0:256] = wo[...].astype(F32).T.astype(BF16)
        for j in range(8):
            part = wf2[j * 128 : (j + 1) * 128, :].astype(F32).T.astype(BF16)
            wout[wrow, 256 + j * 128 : 256 + (j + 1) * 128] = part

    def begin_of(row):
        e0 = lens[0, 0]
        e1 = e0 + lens[0, 1]
        e2 = e1 + lens[0, 2]
        first = jnp.where(row >= e0, e0, 0)
        return jnp.where(row >= e2, e2, jnp.where(row >= e1, e1, first))

    def tables(i, carry):
        at = rows_at(i * 64, 64)
        row = lax.broadcasted_iota(jnp.int32, (64, 1), 0) + i * 64
        angle = (row - begin_of(row)).astype(F32) * freq[...]
        cos[at, :] = jnp.cos(angle)
        sin[at, :] = jnp.sin(angle) * sign[...]
        return carry

    @step
    def tab():
        lax.fori_loop(0, GROUP // 64, tables, 0)

    lanes = lax.broadcasted_iota(jnp.int32, (1, 128), 1)
    head_mask = (lanes < HD, lanes >= HD)
    first_half = lanes % ROT < ROT // 2

    def turn(values, at, way):
        swapped = jnp.where(first_half, pltpu.roll(values, 112, 1), pltpu.roll(values, 16, 1))
        return values * cos[at, :] + swapped * (sin[at, :] * way)

    def project(half):
        at = rows_at(half * 512, 512)
        xb = x[at, :]
        products = dot_nn(xb, win[:, 0:QKV])
        for t in range(3):
            pre = products[:, t * 256 : (t + 1) * 256] + bq[t : t + 1, :]
            for j in range(2):
                part = pre[:, j * 128 : (j + 1) * 128]
                if t < 2:
                    part = turn(part, at, 1.0)
                if t == 0:
                    part = part * (HD**-0.5 * LOG2E)
                qp[at, t * 256 + j * 128 : t * 256 + (j + 1) * 128] = part.astype(BF16)

        def hidden(j, carry):
            cols = pl.ds(pl.multiple_of(j * 512, 256), 512)
            wcols = pl.ds(pl.multiple_of(QKV + j * 512, 256), 512)
            pre = dot_nn(x[at, :], win[:, wcols]) + b1[:, cols]
            square = pre * pre
            slope = 0.7978845608028654 * (1.0 + 0.134145 * square)
            t = jnp.tanh(0.7978845608028654 * pre * (1.0 + 0.044715 * square))
            half_up = 0.5 * (1.0 + t)
            ah[at, pl.ds(pl.multiple_of(256 + j * 512, 256), 512)] = (pre * half_up).astype(BF16)
            qp[at, wcols] = (half_up + 0.5 * pre * (1.0 - t * t) * slope).astype(BF16)
            return carry

        lax.fori_loop(0, FC // 512, hidden, 0)

    @step
    def proj():
        ci.arrived()
        gx.arrived(5, 7, 8, 9, 10, 11)

        def part(i, carry):
            project(i)
            return carry

        lax.fori_loop(0, 2, part, 0)

    stack = {7: (0, 0), 6: (0, 8), 2: (0, 15), 5: (1, 0), 4: (1, 6), 3: (1, 11), 1: (1, 15), 0: (1, 17)}

    def both(part):
        none = jnp.zeros_like(part)
        return jnp.concatenate([jnp.where(mask, part, none) for mask in head_mask], axis=0)

    def own_parts(product):
        return jnp.concatenate([product[0:HD, 0:128], product[HD:128, 128:256]], axis=0).T

    def kept(pair, i):
        side, row = stack[i]
        cols = pl.ds(pl.multiple_of(pair * 512 + side * 256, 256), 256)
        return pool.at[row * 128 : (row + i + 1) * 128, cols]

    def attend(pair, carry):
        qcols = pl.ds(pl.multiple_of(pair * 128, 128), 128)
        kcols = pl.ds(pl.multiple_of(256 + pair * 128, 128), 128)
        vcols = pl.ds(pl.multiple_of(512 + pair * 128, 128), 128)
        for i in range(4):
            at = pl.ds(i * 256, 256)
            kt[qcols, at] = qp[at, kcols].astype(F32).T.astype(BF16)
            vt[qcols, at] = qp[at, vcols].astype(F32).T.astype(BF16)
        for i in range(8):
            at = pl.ds(i * 128, 128)
            deep = (i + 1) * 128
            key_row = lax.broadcasted_iota(jnp.int32, (deep, 256), 0)
            row = (lax.broadcasted_iota(jnp.int32, (1, 256), 1) & 127) + i * 128
            allowed = (key_row >= begin_of(row)) & (key_row <= row)
            s = jnp.where(allowed, dot_nt(qp[:deep, kcols], both(qp[at, qcols])), -1e30)
            ex = jnp.exp2(s - jnp.max(s, axis=0, keepdims=True))
            probs = (ex * (1.0 / jnp.sum(ex, axis=0, keepdims=True))).astype(BF16)
            kept(pair, i)[...] = probs
            ah[at, qcols] = own_parts(dot_nn(vt[qcols, :deep], probs)).astype(BF16)
        return carry

    transfers("attf", (lax.fori_loop, 0, 2, attend, 0))

    def chunk(src, h, f, a, q, send, recv, c):
        cols = pl.ds(pl.multiple_of(c * CHUNK, CHUNK), CHUNK)
        return RingReduce(
            lambda slot, count: src.at[slot // 2, slot % 2, 0:count, cols],
            mp_slots(),
            who,
            ("xx", "yp", "ym"),
            lambda i, count: h.at[i, 0:count, cols],
            lambda i, j, count: f.at[i, j, 0:count, cols],
            a.at[:, cols],
            send.at[c],
            recv.at[c],
            KEEP,
            (
                src.at[:, 1 - xh, KEEP:ROWS, cols],
                q.at[:, :, cols],
                lambda place_on_ring: src.at[place_on_ring, xh, KEEP:ROWS, cols],
            ),
        )

    def r1(c):
        return chunk(p1, h1, f1, a1, q1, r1s, r1r, c)

    def r2(c):
        return chunk(y, h2, f2, a2, q2, r2s, r2r, c)

    def over_dp(src, h, f, a, send, recv, cols):
        return RingReduce(
            lambda slot, count: src.at[rows_at(slot * ROWS, count), cols],
            dp_slots(),
            who,
            ("xl", "zp", "zm"),
            lambda i, count: h.at[i, 0:count, cols],
            lambda i, j, count: f.at[i, j, 0:count, cols],
            a.at[:, cols],
            send,
            recv,
        )

    out_cols, fc_cols, qkv_cols = pl.ds(0, OUT_W), pl.ds(QKV, FC), pl.ds(0, QKV)
    ro = over_dp(wout, ho, fo, ao, ros, ror, out_cols)
    rf = over_dp(win, hi, fi, ai, rfs, rfr, fc_cols)
    rq = over_dp(win, hi, fi, ai, rqs, rqr, qkv_cols)

    def total(src, f, a, at, with_pair):
        terms = [src[yy, xh, at, :], f[0, 0, at, :], f[1, 0, at, :]]
        if with_pair:
            terms.append(a[at, :])
        terms = [term.astype(F32) for term in terms]
        return sum(terms[1:], terms[0])

    def each_row_block(body):
        each(KEEP, lambda at: body(at, True))
        each(ROWS, lambda at: body(at, False), start=KEEP)

    def spread_columns(src, w, dst, reduced, c):
        cols = pl.ds(pl.multiple_of(c * CHUNK, CHUNK), CHUNK)

        def part(i, carry):
            at = rows_at(i * 512, 512)
            product = dot_nt(src[at, :], w[cols, :]).astype(BF16)
            dst[pl.ds(i * 2, 2), :, :, cols] = product.reshape(2, 2, ROWS, CHUNK)
            return carry

        lax.fori_loop(0, GROUP // 512, part, 0)
        reduced(c).start(7, 1, 2)

    def branches(c, carry):
        spread_columns(ah, wout, p1, r1, c)
        return carry

    transfers("p1", (co_.arrived,), (lax.fori_loop, 0, CHUNKS, branches, 0))

    def back_rows(i):
        at = rows_at(i * 512, 512)
        dout[at, :] = dot_nn(y[pl.ds(i * 2, 2)].reshape(512, D), wout[:, 0:256]).astype(BF16)

        def hidden(j, carry):
            wcols = pl.ds(pl.multiple_of(256 + j * 512, 256), 512)
            cols = pl.ds(pl.multiple_of(QKV + j * 512, 256), 512)
            grad = dot_nn(y[pl.ds(i * 2, 2)].reshape(512, D), wout[:, wcols])
            qp[at, cols] = (grad * qp[at, cols].astype(F32)).astype(BF16)
            return carry

        lax.fori_loop(0, FC // 512, hidden, 0)

    @step
    def backs():
        gy.arrived(5, 7, 8, 9, 10, 11)

        def part(i, carry):
            back_rows(i)
            return carry

        lax.fori_loop(0, 2, part, 0)
        for item in (gi, go, ci, co_, gy, gx):
            item.sent()

    def crossing(dst, landing_of, cols, send, recv):
        copies, takes = [], []
        for n, step in enumerate((2, 1, 3, 0)):
            for two in range(2):
                slot = ((z + step) % 4) * 4 + two * 2 + core
                other = slot + 1 - 2 * core
                i = 2 * n + two
                landing = landing_of(i)
                copies.append(
                    remote(dst.at[rows_at(other * ROWS, ROWS), cols], landing, send.at[i], recv.at[i], who["core"])
                )
                takes.append((dst.at[rows_at(slot * ROWS, ROWS), cols], landing))
        return copies, takes

    def landing_out(i):
        return co.at[rows_at(i * ROWS, ROWS)]

    def landing_fc(i):
        return pool.at[rows_at(i * ROWS, ROWS)]

    def landing_qkv(i):
        return pool.at[rows_at(GROUP + i * ROWS, ROWS), 0:QKV]

    out_copies, out_takes = crossing(wout, landing_out, out_cols, kos, kor)
    fc_copies, fc_takes = crossing(win, landing_fc, fc_cols, kfs, kfr)
    qkv_copies, qkv_takes = crossing(win, landing_qkv, qkv_cols, kqs, kqr)

    def take(copies, takes, *which):
        for i in which:
            copies[i].wait_recv()
            add_into(*takes[i])

    def weight_grad(act, grad, dst, n, *copies):
        base = ((z + (2, 1, 3, 0)[n]) % 4) * 512

        def part(two, carry):
            cols = pl.ds(pl.multiple_of(base + two * 256, 256), 256)
            dst[cols, :] = dot_tn(act(cols), grad[...]).astype(BF16)
            return carry

        lax.fori_loop(0, 2, part, 0)
        for some in copies:
            some[2 * n].start()
            some[2 * n + 1].start()

    def x_cols(cols):
        return x[:, cols]

    def y_cols(cols):
        return y[:, :, :, cols].reshape(GROUP, 256)

    for n in range(4):
        transfers(f"dwo{n}", (weight_grad, y_cols, ah, wout, n, out_copies))
        transfers(f"dwi{n}", (weight_grad, x_cols, qp, win, n, fc_copies, qkv_copies))
    for name, copies, takes, ring in (
        ("ko", out_copies, out_takes, ro),
        ("kf", fc_copies, fc_takes, rf),
        ("kq", qkv_copies, qkv_takes, rq),
    ):
        for n, go_on in enumerate(((0, 1), (2,), (3,), ())):
            transfers(f"{name}.t{n}", (take, copies, takes, 2 * n, 2 * n + 1), (ring.start, *go_on))
    for name, ring in (("ro", ro), ("rf", rf), ("rq", rq)):
        transfers(f"{name}.s1a", (ring.up_term,))
        transfers(f"{name}.s1b", (ring.down_term,))
        transfers(f"{name}.th", (ring.third,))
    for name, ring in (("r1", r1), ("r2", r2)):
        for c in range(CHUNKS):
            part = ring(c)
            transfers(f"{name}{c}_qa", (part.add_rest,), (part.start, 0, 3))
            transfers(f"{name}{c}_s1a", (part.up_term,))
            transfers(f"{name}{c}_s1b", (part.down_term,))
            transfers(f"{name}{c}_th", (part.third,))

    def attend_back(pair):
        qcols = pl.ds(pair * 128, 128)
        kcols = pl.ds(256 + pair * 128, 128)
        vcols = pl.ds(512 + pair * 128, 128)
        dk[...] = jnp.zeros_like(dk)
        dv[...] = jnp.zeros_like(dv)
        for i in range(8):
            at = pl.ds(i * 128, 128)
            deep = (i + 1) * 128
            do2 = dout[at, qcols]
            queries, grads = both(qp[at, qcols]), both(do2)
            prod = (do2.astype(F32) * ah[at, qcols].astype(F32)).T
            centre = jnp.concatenate(
                [jnp.sum(prod[h * HD : (h + 1) * HD], axis=0, keepdims=True) for h in range(2)], axis=1
            )
            probs = kept(pair, i)[...]
            ds = (probs.astype(F32) * (dot_nt(qp[:deep, vcols], grads) - centre)).astype(BF16)
            dq = own_parts(dot_nn(kt[qcols, :deep], ds)) * (HD**-0.5)
            dk[:deep, :] += dot_nn(ds, queries)
            dv[:deep, :] += dot_nn(probs, grads)
            qp[at, qcols] = turn(dq, at, -1.0).astype(BF16)
        for i in range(4):
            at = pl.ds(i * 256, 256)
            qp[at, kcols] = turn(dk[at, :] * LN2, at, -1.0).astype(BF16)
            qp[at, vcols] = dv[at, :].astype(BF16)

    transfers("attb0", (attend_back, 0))

    def pool_is_free():
        pl.semaphore_signal(free, inc=1, device_id=who["core"], device_id_type=MESH)

    transfers("attb1", (attend_back, 1), (pool_is_free,))
    for c in range(CHUNKS):
        transfers(f"p2.{c}", (spread_columns, qp, win, y, r2, c))
    transfers("pool", (pl.semaphore_wait, free, 1))

    def mix_rows(at, with_pair):
        branches = total(p1, f1, a1, at, with_pair)
        mixed[at, :] = (tokens[at, :].astype(F32) + branches + (bo[...] + b2[...])).astype(BF16)

    @step
    def mix():
        for c in range(CHUNKS):
            r1(c).arrived()
        each_row_block(mix_rows)
        send_out(0, *outputs[0])

    @step
    def bias():
        def part(i, carry):
            at = rows_at(i * 128, 128)
            sums = jnp.sum(qp[at, :].astype(F32), axis=0, keepdims=True)
            small[6:7, :] += sums[:, 0:1024]
            small[7:8, 0:QKV] += sums[:, 1024:IN_W]
            return carry

        small[...] = jnp.zeros_like(small)
        lax.fori_loop(0, 8, part, 0)

    def norm_of(at):
        values = tokens[at, :].astype(F32)
        center = values - jnp.mean(values, axis=-1, keepdims=True)
        rstd = lax.rsqrt(jnp.mean(center * center, axis=-1, keepdims=True) + 1e-05)
        return center * rstd, rstd

    def sums_of(at, with_pair):
        ngrad = total(y, f2, a2, at, with_pair)
        for n, term in enumerate((ngrad * norm_of(at)[0], ngrad, cot[at, :].astype(F32))):
            sums = jnp.sum(term, axis=0, keepdims=True)
            small[2 * n : 2 * n + 1, :] += sums[:, 0:1024]
            small[2 * n + 1 : 2 * n + 2, :] += sums[:, 1024:2048]

    def around(n, buffer, here, names, places):
        buffer[here] = small[...]
        copies = []
        for k, name in enumerate(names):
            i = n + k
            copies.append(remote(buffer.at[here], buffer.at[here], sms.at[i], smr.at[i], who[name]))
            copies[-1].start()

        def finish():
            for k, name in enumerate(names):
                there = buffer.at[places[k]]
                remote(there, there, sms.at[n + k], smr.at[n + k], who[name]).wait_recv()
            for c in copies:
                c.wait_send()

        return finish

    xi = xh * 2 + xl
    along_x = [((xi + way) % 4) * 2 for way in (3, 1, 2)]
    rounds = {}

    @step
    def sums():
        for c in range(CHUNKS):
            r2(c).arrived()
        each_row_block(sums_of)
        rounds["x"] = around(
            0,
            got_x,
            xi * 2 + core,
            ("core", "xp", "xm", "xx", "xp2", "xm2", "xx2"),
            [xi * 2 + 1 - core] + [p + core for p in along_x] + [p + 1 - core for p in along_x],
        )

    def back_norm(at, with_pair):
        xhat, rstd = norm_of(at)
        ex = total(y, f2, a2, at, with_pair) * gain[...]
        mean_e = jnp.mean(ex, axis=-1, keepdims=True)
        mean_ex = jnp.mean(ex * xhat, axis=-1, keepdims=True)
        tgrad[at, :] = (cot[at, :].astype(F32) + (ex - mean_e - xhat * mean_ex) * rstd).astype(BF16)

    transfers("back", (each_row_block, back_norm), (send_out, 1, *outputs[1]))

    @step
    def sum_x():
        rounds["x"]()
        small[0:6, :] = jnp.sum(got_x[:, 0:6, :], axis=0)
        small[6:8, :] = jnp.sum(got_x[pl.ds(4 * xh, 4), 6:8, :], axis=0)
        rounds["z"] = around(7, got.at[0], z, ("zp", "zm", "zz"), [(z + way) % 4 for way in (3, 1, 2)])

    @step
    def sum_z():
        rounds["z"]()
        small[...] = jnp.sum(got[0], axis=0)
        rounds["y"] = around(10, got.at[1], yy, ("yp", "ym", "yy"), [(yy + way) % 4 for way in (3, 1, 2)])

    @step
    def sum_y():
        rounds["y"]()
        small[0:6, :] = jnp.sum(got[1, :, 0:6, :], axis=0)

    @step
    def lasto():
        def rows(at):
            gout[at, :] = ro.total(at)

        ro.arrived()
        each(ROWS, rows)
        send_out(3, *outputs[3])

    @step
    def lastf():
        def rows(at):
            gin[at, QKV:IN_W] = rf.total(at)

        rf.arrived()
        each(ROWS, rows)

    @step
    def lastq():
        def rows(at):
            gin[at, 0:QKV] = rq.total(at)

        rq.arrived()
        each(ROWS, rows)

    for name in ORDER:
        steps[name]()
    send_out(2, *outputs[2])
    send_out(4, *outputs[4])

    for c in range(CHUNKS):
        r1(c).sent()
        r2(c).sent()
    for r in (ro, rf, rq):
        r.sent()
    for c in out_copies + fc_copies + qkv_copies:
        c.wait_send()
    for index, (src, dst) in enumerate(outputs):
        pltpu.make_async_copy(src, dst, out_of.at[index]).wait()


def block(*args):
    sems = pltpu.SemaphoreType.DMA

    def low(*shape):
        return pltpu.VMEM(shape, BF16)

    ring = [low(2, ROWS, D), low(2, 2, ROWS, D), low(KEEP, D), low(4, ROWS - KEEP, D)]
    rows_4d = low(4, 2, ROWS, D)
    smem = pl.BlockSpec(memory_space=pltpu.SMEM)
    return pl.pallas_call(
        block_kernel,
        out_shape=(
            jax.ShapeDtypeStruct((ROWS, D), BF16),
            jax.ShapeDtypeStruct((ROWS, D), BF16),
            jax.ShapeDtypeStruct((ROWS, IN_W), F32),
            jax.ShapeDtypeStruct((ROWS, OUT_W), F32),
            jax.ShapeDtypeStruct((8, 1024), F32),
        ),
        in_specs=[ANY, ANY, smem, ANY, VMEM, ANY, VMEM, ANY, VMEM, ANY] + [VMEM] * 5,
        out_specs=(ANY,) * 5,
        scratch_shapes=[
            low(ROWS, D), low(ROWS, D), low(256, ROWS), low(FC, ROWS),
            pltpu.VMEM((ROWS, IN_W), F32), pltpu.VMEM((ROWS, OUT_W), F32), pltpu.VMEM((8, 1024), F32),
            sems((9,)), sems((5,)),
            low(GROUP, D), rows_4d, low(D, IN_W), low(D, OUT_W),
            low(GROUP, OUT_W), low(GROUP, IN_W), low(GROUP, 256), low(2560, GROUP), rows_4d,
            pltpu.VMEM((GROUP, 128), F32), pltpu.VMEM((GROUP, 128), F32),
            pltpu.VMEM((GROUP, 128), F32), pltpu.VMEM((GROUP, 128), F32),
            *ring, *ring,
            low(2, ROWS, IN_W), low(2, 2, ROWS, IN_W), low(ROWS, IN_W),
            low(2, ROWS, OUT_W), low(2, 2, ROWS, OUT_W), low(ROWS, OUT_W),
            low(8 * ROWS, OUT_W),
            pltpu.VMEM((8, 8, 1024), F32), pltpu.VMEM((2, 4, 8, 1024), F32),
            low(256, GROUP), low(256, GROUP),
            sems((12,)), sems((12,)), sems((12,)), sems((12,)),
            sems((9,)), sems((9,)), sems((10,)), sems((10,)),
            sems((9,)), sems((9,)), sems((10,)), sems((10,)),
            sems((CHUNKS, 8)), sems((CHUNKS, 8)), sems((CHUNKS, 8)), sems((CHUNKS, 8)),
            sems((7,)), sems((7,)), sems((7,)), sems((7,)), sems((7,)), sems((7,)),
            sems((8,)), sems((8,)), sems((8,)), sems((8,)), sems((8,)), sems((8,)),
            sems((13,)), sems((13,)), pltpu.SemaphoreType.REGULAR,
        ],
        compiler_params=pltpu.CompilerParams(
            collective_id=0, has_side_effects=True, vmem_limit_bytes=VMEM_LIMIT
        ),
        name="block",
    )(*args)


def finish_kernel(
    mixed, tgrad, gin, gout, small,
    o_mixed, o_tgrad, gq, bq, go, bo, g1, b1, g2, b2, gain, shift,
    kept, sums, sem,
):
    def copy(index, src, dst):
        c = pltpu.make_async_copy(src, dst, sem.at[index])
        c.start()
        return c

    out, totals = copy(0, gout, kept), copy(1, small, sums)
    rest = [copy(2, mixed, o_mixed), copy(3, tgrad, o_tgrad), copy(4, gin.at[:, QKV:IN_W], g1)]
    for t in range(3):
        rest.append(copy(5 + t, gin.at[:, t * 256 : (t + 1) * 256], gq.at[t]))
    totals.wait()
    for t in range(3):
        bq[t : t + 1, :] = sums[6:7, t * 256 : (t + 1) * 256]
    b1[:, 0:256] = sums[6:7, QKV:1024]
    b1[:, 256:FC] = sums[7:8, 0:QKV]
    for n in range(2):
        cols = slice(n * 1024, (n + 1) * 1024)
        gain[:, cols] = sums[n : n + 1, :]
        shift[:, cols] = sums[2 + n : 3 + n, :]
        bo[:, cols] = sums[4 + n : 5 + n, :]
        b2[:, cols] = sums[4 + n : 5 + n, :]
    out.wait()
    go[...] = kept[:, 0:256].T
    for j in range(8):
        g2[j * 128 : (j + 1) * 128, :] = kept[:, 256 + j * 128 : 256 + (j + 1) * 128].T
    for c in rest:
        c.wait()


def finish(*args):
    def out(*shape):
        return jax.ShapeDtypeStruct(shape, F32)

    rows = jax.ShapeDtypeStruct((ROWS, D), BF16)
    shapes = (
        rows, rows, out(3, ROWS, 256), out(3, 256), out(256, ROWS), out(1, D), out(ROWS, FC), out(1, FC),
        out(FC, ROWS), out(1, D), out(1, D), out(1, D),
    )
    return pl.pallas_call(
        finish_kernel,
        out_shape=shapes,
        in_specs=[ANY] * 5,
        out_specs=(VMEM,) * 12,
        scratch_shapes=[
            pltpu.VMEM((ROWS, OUT_W), F32), pltpu.VMEM((8, 1024), F32), pltpu.SemaphoreType.DMA((8,))
        ],
        compiler_params=pltpu.CompilerParams(vmem_limit_bytes=VMEM_LIMIT),
        name="finish",
    )(*args)


def per_device(
    tokens, cotangent, seq_lengths, w_qkv, b_qkv, w_out, b_out, w_fc1, b_fc1, w_fc2, b_fc2, ln_gain, ln_bias
):
    lane = np.arange(128) % HD
    angle = np.float32(10000.0) ** (np.float32(-2.0) * (lane % (ROT // 2)).astype(np.float32) / np.float32(ROT))
    freq = jnp.asarray(np.where(lane < ROT, angle, 0.0).astype(np.float32))
    sign = jnp.asarray(np.where(lane < ROT // 2, -1.0, np.where(lane < ROT, 1.0, 0.0)).astype(np.float32))
    parts = block(
        tokens, cotangent, seq_lengths, jnp.transpose(w_qkv, (1, 0, 2)), b_qkv, w_out, b_out[None], w_fc1,
        b_fc1[None], w_fc2, b_fc2[None], ln_gain[None], ln_bias[None], freq[None], sign[None],
    )
    mixed, tgrad, gq, bq, go, bo, g1, b1, g2, b2, gain, shift = finish(*parts)
    return (
        mixed, tgrad, jnp.transpose(gq, (1, 0, 2)), bq, go, bo[0], g1, b1[0], g2, b2[0], gain[0], shift[0]
    )


def solution(mesh):
    in_specs = (
        P(("dp", "mp"), None),
        P(("dp", "mp"), None),
        P("dp", None),
        P("dp", None, "mp"),
        P(None, "mp"),
        P("mp", "dp"),
        P(),
        P("dp", "mp"),
        P("mp"),
        P("mp", "dp"),
        P(),
        P(),
        P(),
    )
    out_specs = (
        P(("dp", "mp"), None),
        P(("dp", "mp"), None),
        P("dp", None, "mp"),
        P(None, "mp"),
        P("mp", "dp"),
        P(),
        P("dp", "mp"),
        P("mp"),
        P("mp", "dp"),
        P(),
        P(),
        P(),
    )
    return jax.shard_map(
        per_device, mesh=mesh, in_specs=in_specs, out_specs=out_specs, check_vma=False
    )
```

```python
import jax
import jax.numpy as jnp
import numpy as np
from jax import lax
from jax.experimental import pallas as pl
from jax.experimental.pallas import tpu as pltpu
from jax.sharding import PartitionSpec as P

HD = 64
ROT = 32
MESH = pl.DeviceIdType.MESH
BF16 = jnp.bfloat16
F32 = jnp.float32
ROWS = 128
GROUP = 1024
D = 2048
QKV = 768
FC = 1024
IN_W = QKV + FC
OUT_W = 256 + FC
ALL_W = IN_W + OUT_W
LOG2E = 1.4426950408889634
LN2 = 0.6931471805599453
CHUNKS = 4
CHUNK = D // CHUNKS
KEEP = 96
VMEM_LIMIT = 64 * 1024 * 1024 - 65536

ORDER = (
    "Wi.go", "ln", "X.go", "X.x", "wprep", "tab", "Wi.f1", "X.f1", "Wi.p", "Wi.c1", "Y.x", "X.p", "X.q1", "X.q2",
    "Wi.f2", "Wi.c2", "Wo.go", "Wo.x", "X.f2", "Y.go", "Wi.c3", "Wo.f1", "proj", "Y.f1", "Y.q1", "Y.p", "Wo.p",
    "Wo.c1", "attf", "Wo.f2", "Wo.c2", "Y.q2", "Wo.c3", "Y.f2", "p1", "r10_qa", "backs", "r10_s1b", "r11_qa",
    "r11_s1b", "r12_qa", "r13_qa", "dwo0", "r10_s1a", "dwo1", "dwo2", "ko.t0", "dwo3", "ko.t1", "attb0", "r10_th",
    "r11_s1a", "r12_s1a", "r12_s1b", "ko.t2", "ko.t3", "ro.s1b", "attb1", "r11_th", "r12_th", "r13_s1a", "r13_s1b",
    "ro.s1a", "bias", "p2.0", "p2.1", "r13_th", "p2.2", "r20_s1b", "ro.th", "p2.3", "r20_qa", "r21_s1b", "pool",
    "dwi0", "dwi1", "mix", "r20_s1a", "r21_qa", "kq.t0", "dwi2", "r22_qa", "kf.t0", "kf.t1", "r23_qa", "kq.t1",
    "dwi3", "kq.t2", "kf.t2", "rq.s1b", "rq.s1a", "r20_th", "r22_s1b", "r21_s1a", "kq.t3", "kf.t3", "r22_s1a",
    "r21_th", "r23_s1a", "r23_s1b", "r22_th", "rf.s1b", "r23_th", "rf.s1a", "sums", "rq.th", "lasto", "back",
    "rf.th", "sum_x", "sum_z", "sum_y", "lastq", "lastf",
)

VMEM = pl.BlockSpec(memory_space=pltpu.VMEM)
ANY = pl.BlockSpec(memory_space=pl.ANY)


def place():
    dp = lax.axis_index("dp")
    mp = lax.axis_index("mp")
    return dp, mp


def peers():
    dp, mp = place()
    z, low = dp // 4, dp % 4
    y, xh = mp // 2, mp % 2
    core = low % 2
    xl = low // 2
    flipped = z * 4 + (1 - xl) * 2 + core
    return {
        "core": (z * 4 + xl * 2 + (1 - core), mp),
        "xp": (flipped, y * 2 + (xh + xl) % 2),
        "xm": (flipped, y * 2 + (xh + 1 - xl) % 2),
        "xx": (dp, y * 2 + (1 - xh)),
        "xl": (flipped, mp),
        "xp2": (flipped + 1 - 2 * core, y * 2 + (xh + xl) % 2),
        "xm2": (flipped + 1 - 2 * core, y * 2 + (xh + 1 - xl) % 2),
        "xx2": (dp + 1 - 2 * core, y * 2 + (1 - xh)),
        "zp": (((z + 1) % 4) * 4 + low, mp),
        "zm": (((z + 3) % 4) * 4 + low, mp),
        "zz": (((z + 2) % 4) * 4 + low, mp),
        "yp": (dp, ((y + 1) % 4) * 2 + xh),
        "ym": (dp, ((y + 3) % 4) * 2 + xh),
        "yy": (dp, ((y + 2) % 4) * 2 + xh),
    }


class remote:
    def __init__(self, src, dst, send, recv, target):
        self.parts = dict(
            src_ref=src, dst_ref=dst, send_sem=send, recv_sem=recv, device_id=target, device_id_type=MESH
        )

    def start(self):
        pltpu.make_async_remote_copy(**self.parts).start()

    def wait(self):
        pltpu.make_async_remote_copy(**self.parts).wait()

    def wait_send(self):
        pltpu.make_async_remote_copy(**self.parts).wait_send()

    def wait_recv(self):
        pltpu.make_async_remote_copy(**self.parts).wait_recv()


def rows_at(start, count):
    return pl.ds(pl.multiple_of(start, 16), count)


def mp_slots():
    _, mp = place()
    y, xh = mp // 2, mp % 2

    def at(step):
        base = ((y + step) % 4) * 2
        return (base + xh, base + (1 - xh))

    return mp, at(0)[1], at(1), at(3), at(2)


def dp_slots():
    dp, _ = place()
    z, xl, core = dp // 4, (dp // 2) % 2, dp % 2

    def at(step):
        base = ((z + step) % 4) * 4 + core
        return (base + xl * 2, base + (1 - xl) * 2)

    return dp, at(0)[1], at(1), at(3), at(2)


class RingGather:
    def __init__(self, piece, slots, pair, up, down, send, recv, keep=ROWS):
        slot, pair_slot, plus, minus, opposite = slots
        half, mid = ROWS // 2, keep // 2

        def copy(index, which, target, start=0, count=ROWS):
            part = piece(which, start, count)
            return remote(part, part, send.at[index], recv.at[index], target)

        self.go = [
            copy(0, slot, pair),
            copy(1, slot, up),
            copy(2, slot, down),
            copy(3, pair_slot, up, 0, keep),
            copy(4, pair_slot, down, 0, keep),
            copy(5, minus[0], up, 0, half),
            copy(6, plus[0], down, half, half),
            copy(7, minus[1], up, 0, mid),
            copy(8, plus[1], down, mid, mid),
        ]
        self.come = [
            copy(0, pair_slot, pair),
            copy(1, minus[0], up),
            copy(2, plus[0], down),
            copy(3, minus[1], up, 0, keep),
            copy(4, plus[1], down, 0, keep),
            copy(5, opposite[0], up, 0, half),
            copy(6, opposite[0], down, half, half),
            copy(7, opposite[1], up, 0, mid),
            copy(8, opposite[1], down, mid, mid),
        ]
        if keep < ROWS:
            for index, two in ((9, minus), (10, plus), (11, opposite)):
                self.go.append(copy(index, two[0], pair, keep, ROWS - keep))
                self.come.append(copy(index, two[1], pair, keep, ROWS - keep))

    def start(self, *which):
        for i in which:
            self.go[i].start()

    def arrived(self, *which):
        for i in which:
            self.come[i].wait_recv()

    def sent(self):
        for c in self.go:
            c.wait_send()


class CoreShare:
    def __init__(self, ref, target, send, recv):
        slot, pair_slot, plus, minus, opposite = dp_slots()
        half = ROWS // 2
        flip = 1 - 2 * (place()[0] % 2)
        pieces = [
            (pair_slot, 0, ROWS),
            (minus[0], 0, ROWS),
            (plus[0], 0, ROWS),
            (minus[1], 0, ROWS),
            (plus[1], 0, ROWS),
            (opposite[0], 0, half),
            (opposite[0], half, half),
            (opposite[1], 0, half),
            (opposite[1], half, half),
            (slot, 0, ROWS),
        ]

        def copy(index, which, start, count):
            piece = ref.at[rows_at(which * ROWS + start, count)]
            return remote(piece, piece, send.at[index], recv.at[index], target)

        self.go = [copy(i, s, a, n) for i, (s, a, n) in enumerate(pieces)]
        self.come = [copy(i, s + flip, a, n) for i, (s, a, n) in enumerate(pieces)]

    def start(self, *which):
        for i in which:
            self.go[i].start()

    def arrived(self):
        for c in self.come:
            c.wait_recv()

    def sent(self):
        for c in self.go:
            c.wait_send()


def each(count, body, size=16, start=0):
    def step(i, carry):
        body(pl.ds(pl.multiple_of(i * size, size), size))
        return carry

    lax.fori_loop(start // size, count // size, step, 0)


def add_into(dst, term):
    def body(at):
        dst[at, :] = dst[at, :] + term[at, :]

    each(dst.shape[0], body, 32)


class RingReduce:
    def __init__(self, part, slots, who, names, half, full, across, send, recv, keep=ROWS, rest=()):
        slot, pair_slot, plus, minus, opposite = slots
        pair, up, down = (who[name] for name in names)
        self.part, self.slot, self.full, self.across = part, slot, full, across
        self.half, self.keep = half, keep
        self.pair_part = part(pair_slot, keep)
        self.plus_own, self.minus_pair = part(plus[0], ROWS), part(minus[1], keep)

        def go(index, src, dst, target):
            return remote(src, dst, send.at[index], recv.at[index], target)

        self.sends = [
            go(0, part(opposite[0], ROWS), half(0, ROWS), up),
            go(1, part(opposite[1], keep), half(1, keep), down),
            go(2, part(plus[1], keep), full(0, 1, keep), up),
            go(3, part(minus[0], ROWS), full(1, 0, ROWS), down),
            go(4, self.plus_own, full(0, 0, ROWS), up),
            go(5, self.minus_pair, full(1, 1, keep), down),
            go(6, self.pair_part, across, pair),
        ]
        if rest:
            rest_of, self.rest, self.rest_at = rest
            self.sends.append(go(7, rest_of, self.rest, pair))

    def start(self, *which):
        for i in which:
            self.sends[i].start()

    def add_rest(self):
        self.sends[7].wait_recv()
        for place_on_ring in range(4):
            add_into(self.rest_at(place_on_ring), self.rest.at[place_on_ring])

    def up_term(self):
        self.sends[0].wait_recv()
        add_into(self.plus_own, self.half(0, ROWS))
        self.start(4)

    def down_term(self):
        self.sends[1].wait_recv()
        add_into(self.minus_pair, self.half(1, self.keep))
        self.start(5)

    def third(self):
        for i in (2, 3, 4, 5):
            self.sends[i].wait_recv()
        dst, a, b = self.pair_part, self.full(0, 1, self.keep), self.full(1, 1, self.keep)

        def body(at):
            total = dst[at, :].astype(F32) + a[at, :].astype(F32) + b[at, :].astype(F32)
            dst[at, :] = total.astype(dst.dtype)

        each(self.keep, body, 32)
        self.start(6)

    def arrived(self):
        self.sends[6].wait_recv()

    def total(self, at):
        return (
            self.part(self.slot, ROWS)[at, :].astype(F32)
            + self.full(0, 0, ROWS)[at, :].astype(F32)
            + self.full(1, 0, ROWS)[at, :].astype(F32)
            + self.across[at, :].astype(F32)
        )

    def sent(self):
        for c in self.sends:
            c.wait_send()


def dot_nn(a, b):
    return jnp.dot(a, b, preferred_element_type=F32)


def dot_nt(a, b):
    return lax.dot_general(a, b, (((1,), (1,)), ((), ())), preferred_element_type=F32)


def dot_tn(a, b):
    return lax.dot_general(a, b, (((0,), (0,)), ((), ())), preferred_element_type=F32)


def block_kernel(
    tokens_in, cot_in, lens, wq, bq, wo_in, bo, wf1, b1, wf2_in, b2, gain, shift, freq, sign,
    mixed_out, tgrad_out, gin_out, gout_out, small_out,
    tokens, cot, wo, wf2, gin, gout, small, into, out_of,
    x, y, win, wout, ah, qp, dout, pool, p1, cos, sin, dk, dv,
    h1, f1, a1, q1, h2, f2, a2, q2, hi, fi, ai, ho, fo, ao, co, got_x, got, kt, vt,
    xs, xr, ys, yr, wis, wir, cis, cir, wos, wor, cos_s, cos_r,
    r1s, r1r, r2s, r2r, rfs, rfr, rqs, rqr, ros, ror, kfs, kfr, kqs, kqr, kos, kor, sms, smr, free,
):
    who = peers()
    dp, mp = place()
    core, xl, xh = dp % 2, (dp // 2) % 2, mp % 2
    z, yy = dp // 4, mp // 2
    barrier = pltpu.get_barrier_semaphore()
    met = [who[n] for n in ("core", "xp", "xm", "xx", "xp2", "xm2", "xx2", "zp", "zm", "zz", "yp", "ym", "yy")]
    for target in met:
        pl.semaphore_signal(barrier, inc=1, device_id=target, device_id_type=MESH)

    wrow = rows_at(dp * ROWS, ROWS)
    brought = [(wq.at[t], win.at[wrow, t * 256 : (t + 1) * 256]) for t in range(3)]
    brought += [(wf1, win.at[wrow, QKV:IN_W]), (tokens_in, tokens), (wo_in, wo), (wf2_in, wf2)]
    brought += [(cot_in, cot), (cot_in, y.at[yy, xh])]
    brought = [pltpu.make_async_copy(src, dst, into.at[i]) for i, (src, dst) in enumerate(brought)]
    for c in brought:
        c.start()

    def bring(*which):
        for i in which:
            brought[i].wait()

    def send_out(index, src, dst):
        pltpu.make_async_copy(src, dst, out_of.at[index]).start()

    mixed, tgrad = p1.at[yy, xh], y.at[yy, xh]
    outputs = ((mixed, mixed_out), (tgrad, tgrad_out), (gin, gin_out), (gout, gout_out), (small, small_out))
    pl.semaphore_wait(barrier, len(met))

    def flat(ref):
        return lambda slot, start, count: ref.at[rows_at(slot * ROWS + start, count)]

    def deep(ref):
        return lambda slot, start, count: ref.at[slot // 2, slot % 2, start : start + count]

    gx = RingGather(flat(x), mp_slots(), who["xx"], who["yp"], who["ym"], xs, xr, KEEP)
    gy = RingGather(deep(y), mp_slots(), who["xx"], who["yp"], who["ym"], ys, yr, KEEP)
    gi = RingGather(flat(win), dp_slots(), who["xl"], who["zp"], who["zm"], wis, wir)
    go = RingGather(flat(wout), dp_slots(), who["xl"], who["zp"], who["zm"], wos, wor)
    ci = CoreShare(win, who["core"], cis, cir)
    co_ = CoreShare(wout, who["core"], cos_s, cos_r)
    steps = {}

    def step(function):
        steps[function.__name__] = function
        return function

    def transfers(name, *actions):
        def act():
            for action, *which in actions:
                action(*which)

        steps[name] = act

    transfers("Wi.go", (bring, 0, 1, 2, 3), (gi.start, 1, 2, 0), (ci.start, 9))
    transfers("Wi.p", (gi.arrived, 0), (gi.start, 3, 4))
    transfers("Wi.f1", (gi.arrived, 1), (gi.start, 5), (gi.arrived, 2), (gi.start, 6))
    transfers("Wi.f2", (gi.arrived, 3), (gi.start, 7), (gi.arrived, 4), (gi.start, 8))
    transfers("Wi.c1", (ci.start, 0, 1, 2))
    transfers("Wi.c2", (ci.start, 3, 4))
    transfers("Wi.c3", (gi.arrived, 5, 6, 7, 8), (ci.start, 5, 6, 7, 8))
    transfers("Wo.go", (go.start, 1, 2), (co_.start, 9))
    transfers("Wo.x", (go.start, 0))
    transfers("Wo.p", (go.arrived, 0), (go.start, 3, 4))
    transfers("Wo.f1", (go.arrived, 1), (go.start, 5), (go.arrived, 2), (go.start, 6))
    transfers("Wo.f2", (go.arrived, 3), (go.start, 7), (go.arrived, 4), (go.start, 8))
    transfers("Wo.c1", (co_.start, 0, 1, 2))
    transfers("Wo.c2", (co_.start, 3, 4))
    transfers("Wo.c3", (go.arrived, 5, 6, 7, 8), (co_.start, 5, 6, 7, 8))
    for name, ring in (("X", gx), ("Y", gy)):
        transfers(f"{name}.p", (ring.arrived, 0), (ring.start, 3, 4))
        transfers(f"{name}.f1", (ring.arrived, 1), (ring.start, 5), (ring.arrived, 2), (ring.start, 6))
        transfers(f"{name}.f2", (ring.arrived, 3), (ring.start, 7), (ring.arrived, 4), (ring.start, 8))
        transfers(f"{name}.q1", (ring.start, 9, 10))
        transfers(f"{name}.q2", (ring.arrived, 6), (ring.start, 11))
    transfers("X.go", (gx.start, 1, 2))
    transfers("X.x", (gx.start, 0))
    transfers("Y.go", (gy.start, 1, 2))
    transfers("Y.x", (gy.start, 0))

    def norm_rows(i, carry):
        at = pl.ds(pl.multiple_of(i * 16, 16), 16)
        values = tokens[at, :].astype(F32)
        center = values - jnp.mean(values, axis=-1, keepdims=True)
        spread = jnp.mean(center * center, axis=-1, keepdims=True)
        normed = center * lax.rsqrt(spread + 1e-05) * gain[...] + shift[...]
        x[rows_at(mp * ROWS + i * 16, 16), :] = normed.astype(BF16)
        return carry

    @step
    def ln():
        bring(4)
        lax.fori_loop(0, ROWS // 16, norm_rows, 0)

    @step
    def wprep():
        bring(5, 6, 7, 8)
        wout[wrow, 0:256] = wo[...].astype(F32).T.astype(BF16)
        for j in range(8):
            part = wf2[j * 128 : (j + 1) * 128, :].astype(F32).T.astype(BF16)
            wout[wrow, 256 + j * 128 : 256 + (j + 1) * 128] = part

    def begin_of(row):
        e0 = lens[0, 0]
        e1 = e0 + lens[0, 1]
        e2 = e1 + lens[0, 2]
        first = jnp.where(row >= e0, e0, 0)
        return jnp.where(row >= e2, e2, jnp.where(row >= e1, e1, first))

    def tables(i, carry):
        at = rows_at(i * 64, 64)
        row = lax.broadcasted_iota(jnp.int32, (64, 1), 0) + i * 64
        angle = (row - begin_of(row)).astype(F32) * freq[...]
        cos[at, :] = jnp.cos(angle)
        sin[at, :] = jnp.sin(angle) * sign[...]
        return carry

    @step
    def tab():
        lax.fori_loop(0, GROUP // 64, tables, 0)

    lanes = lax.broadcasted_iota(jnp.int32, (1, 128), 1)
    head_mask = (lanes < HD, lanes >= HD)
    first_half = lanes % ROT < ROT // 2

    def turn(values, at, way):
        swapped = jnp.where(first_half, pltpu.roll(values, 112, 1), pltpu.roll(values, 16, 1))
        return values * cos[at, :] + swapped * (sin[at, :] * way)

    def project(half):
        at = rows_at(half * 512, 512)
        xb = x[at, :]
        products = dot_nn(xb, win[:, 0:QKV])
        for t in range(3):
            pre = products[:, t * 256 : (t + 1) * 256] + bq[t : t + 1, :]
            for j in range(2):
                part = pre[:, j * 128 : (j + 1) * 128]
                if t < 2:
                    part = turn(part, at, 1.0)
                if t == 0:
                    part = part * (HD**-0.5 * LOG2E)
                qp[at, t * 256 + j * 128 : t * 256 + (j + 1) * 128] = part.astype(BF16)

        def hidden(j, carry):
            cols = pl.ds(pl.multiple_of(j * 512, 256), 512)
            wcols = pl.ds(pl.multiple_of(QKV + j * 512, 256), 512)
            pre = dot_nn(x[at, :], win[:, wcols]) + b1[:, cols]
            square = pre * pre
            slope = 0.7978845608028654 * (1.0 + 0.134145 * square)
            t = jnp.tanh(0.7978845608028654 * pre * (1.0 + 0.044715 * square))
            half_up = 0.5 * (1.0 + t)
            ah[at, pl.ds(pl.multiple_of(256 + j * 512, 256), 512)] = (pre * half_up).astype(BF16)
            qp[at, wcols] = (half_up + 0.5 * pre * (1.0 - t * t) * slope).astype(BF16)
            return carry

        lax.fori_loop(0, FC // 512, hidden, 0)

    @step
    def proj():
        ci.arrived()
        gx.arrived(5, 7, 8, 9, 10, 11)

        def part(i, carry):
            project(i)
            return carry

        lax.fori_loop(0, 2, part, 0)

    stack = {7: (0, 0), 6: (0, 8), 2: (0, 15), 5: (1, 0), 4: (1, 6), 3: (1, 11), 1: (1, 15), 0: (1, 17)}

    def both(part):
        none = jnp.zeros_like(part)
        return jnp.concatenate([jnp.where(mask, part, none) for mask in head_mask], axis=0)

    def own_parts(product):
        return jnp.concatenate([product[0:HD, 0:128], product[HD:128, 128:256]], axis=0).T

    def kept(pair, i):
        side, row = stack[i]
        cols = pl.ds(pl.multiple_of(pair * 512 + side * 256, 256), 256)
        return pool.at[row * 128 : (row + i + 1) * 128, cols]

    def attend(pair, carry):
        qcols = pl.ds(pl.multiple_of(pair * 128, 128), 128)
        kcols = pl.ds(pl.multiple_of(256 + pair * 128, 128), 128)
        vcols = pl.ds(pl.multiple_of(512 + pair * 128, 128), 128)
        for i in range(4):
            at = pl.ds(i * 256, 256)
            kt[qcols, at] = qp[at, kcols].astype(F32).T.astype(BF16)
            vt[qcols, at] = qp[at, vcols].astype(F32).T.astype(BF16)
        for i in range(8):
            at = pl.ds(i * 128, 128)
            deep = (i + 1) * 128
            key_row = lax.broadcasted_iota(jnp.int32, (deep, 256), 0)
            row = (lax.broadcasted_iota(jnp.int32, (1, 256), 1) & 127) + i * 128
            allowed = (key_row >= begin_of(row)) & (key_row <= row)
            s = jnp.where(allowed, dot_nt(qp[:deep, kcols], both(qp[at, qcols])), -1e30)
            ex = jnp.exp2(s - jnp.max(s, axis=0, keepdims=True))
            probs = (ex * (1.0 / jnp.sum(ex, axis=0, keepdims=True))).astype(BF16)
            kept(pair, i)[...] = probs
            ah[at, qcols] = own_parts(dot_nn(vt[qcols, :deep], probs)).astype(BF16)
        return carry

    transfers("attf", (lax.fori_loop, 0, 2, attend, 0))

    def chunk(src, h, f, a, q, send, recv, c):
        cols = pl.ds(pl.multiple_of(c * CHUNK, CHUNK), CHUNK)
        return RingReduce(
            lambda slot, count: src.at[slot // 2, slot % 2, 0:count, cols],
            mp_slots(),
            who,
            ("xx", "yp", "ym"),
            lambda i, count: h.at[i, 0:count, cols],
            lambda i, j, count: f.at[i, j, 0:count, cols],
            a.at[:, cols],
            send.at[c],
            recv.at[c],
            KEEP,
            (
                src.at[:, 1 - xh, KEEP:ROWS, cols],
                q.at[:, :, cols],
                lambda place_on_ring: src.at[place_on_ring, xh, KEEP:ROWS, cols],
            ),
        )

    def r1(c):
        return chunk(p1, h1, f1, a1, q1, r1s, r1r, c)

    def r2(c):
        return chunk(y, h2, f2, a2, q2, r2s, r2r, c)

    def over_dp(src, h, f, a, send, recv, cols):
        return RingReduce(
            lambda slot, count: src.at[rows_at(slot * ROWS, count), cols],
            dp_slots(),
            who,
            ("xl", "zp", "zm"),
            lambda i, count: h.at[i, 0:count, cols],
            lambda i, j, count: f.at[i, j, 0:count, cols],
            a.at[:, cols],
            send,
            recv,
        )

    out_cols, fc_cols, qkv_cols = pl.ds(0, OUT_W), pl.ds(QKV, FC), pl.ds(0, QKV)
    ro = over_dp(wout, ho, fo, ao, ros, ror, out_cols)
    rf = over_dp(win, hi, fi, ai, rfs, rfr, fc_cols)
    rq = over_dp(win, hi, fi, ai, rqs, rqr, qkv_cols)

    def total(src, f, a, at, with_pair):
        terms = [src[yy, xh, at, :], f[0, 0, at, :], f[1, 0, at, :]]
        if with_pair:
            terms.append(a[at, :])
        terms = [term.astype(F32) for term in terms]
        return sum(terms[1:], terms[0])

    def each_row_block(body):
        each(KEEP, lambda at: body(at, True))
        each(ROWS, lambda at: body(at, False), start=KEEP)

    def spread_columns(src, w, dst, reduced, c):
        cols = pl.ds(pl.multiple_of(c * CHUNK, CHUNK), CHUNK)

        def part(i, carry):
            at = rows_at(i * 512, 512)
            product = dot_nt(src[at, :], w[cols, :]).astype(BF16)
            dst[pl.ds(i * 2, 2), :, :, cols] = product.reshape(2, 2, ROWS, CHUNK)
            return carry

        lax.fori_loop(0, GROUP // 512, part, 0)
        reduced(c).start(7, 1, 2)

    def branches(c, carry):
        spread_columns(ah, wout, p1, r1, c)
        return carry

    transfers("p1", (co_.arrived,), (lax.fori_loop, 0, CHUNKS, branches, 0))

    def back_rows(i):
        at = rows_at(i * 512, 512)
        dout[at, :] = dot_nn(y[pl.ds(i * 2, 2)].reshape(512, D), wout[:, 0:256]).astype(BF16)

        def hidden(j, carry):
            wcols = pl.ds(pl.multiple_of(256 + j * 512, 256), 512)
            cols = pl.ds(pl.multiple_of(QKV + j * 512, 256), 512)
            grad = dot_nn(y[pl.ds(i * 2, 2)].reshape(512, D), wout[:, wcols])
            qp[at, cols] = (grad * qp[at, cols].astype(F32)).astype(BF16)
            return carry

        lax.fori_loop(0, FC // 512, hidden, 0)

    @step
    def backs():
        gy.arrived(5, 7, 8, 9, 10, 11)

        def part(i, carry):
            back_rows(i)
            return carry

        lax.fori_loop(0, 2, part, 0)
        for item in (gi, go, ci, co_, gy, gx):
            item.sent()

    def crossing(dst, landing_of, cols, send, recv):
        copies, takes = [], []
        for n, step in enumerate((2, 1, 3, 0)):
            for two in range(2):
                slot = ((z + step) % 4) * 4 + two * 2 + core
                other = slot + 1 - 2 * core
                i = 2 * n + two
                landing = landing_of(i)
                copies.append(
                    remote(dst.at[rows_at(other * ROWS, ROWS), cols], landing, send.at[i], recv.at[i], who["core"])
                )
                takes.append((dst.at[rows_at(slot * ROWS, ROWS), cols], landing))
        return copies, takes

    def landing_out(i):
        return co.at[rows_at(i * ROWS, ROWS)]

    def landing_fc(i):
        return pool.at[rows_at(i * ROWS, ROWS)]

    def landing_qkv(i):
        return pool.at[rows_at(GROUP + i * ROWS, ROWS), 0:QKV]

    out_copies, out_takes = crossing(wout, landing_out, out_cols, kos, kor)
    fc_copies, fc_takes = crossing(win, landing_fc, fc_cols, kfs, kfr)
    qkv_copies, qkv_takes = crossing(win, landing_qkv, qkv_cols, kqs, kqr)

    def take(copies, takes, *which):
        for i in which:
            copies[i].wait_recv()
            add_into(*takes[i])

    def weight_grad(act, grad, dst, n, *copies):
        base = ((z + (2, 1, 3, 0)[n]) % 4) * 512

        def part(two, carry):
            cols = pl.ds(pl.multiple_of(base + two * 256, 256), 256)
            dst[cols, :] = dot_tn(act(cols), grad[...]).astype(BF16)
            return carry

        lax.fori_loop(0, 2, part, 0)
        for some in copies:
            some[2 * n].start()
            some[2 * n + 1].start()

    def x_cols(cols):
        return x[:, cols]

    def y_cols(cols):
        return y[:, :, :, cols].reshape(GROUP, 256)

    for n in range(4):
        transfers(f"dwo{n}", (weight_grad, y_cols, ah, wout, n, out_copies))
        transfers(f"dwi{n}", (weight_grad, x_cols, qp, win, n, fc_copies, qkv_copies))
    for name, copies, takes, ring in (
        ("ko", out_copies, out_takes, ro),
        ("kf", fc_copies, fc_takes, rf),
        ("kq", qkv_copies, qkv_takes, rq),
    ):
        for n, go_on in enumerate(((0, 1), (2,), (3,), ())):
            transfers(f"{name}.t{n}", (take, copies, takes, 2 * n, 2 * n + 1), (ring.start, *go_on))
    for name, ring in (("ro", ro), ("rf", rf), ("rq", rq)):
        transfers(f"{name}.s1a", (ring.up_term,))
        transfers(f"{name}.s1b", (ring.down_term,))
        transfers(f"{name}.th", (ring.third,))
    for name, ring in (("r1", r1), ("r2", r2)):
        for c in range(CHUNKS):
            part = ring(c)
            transfers(f"{name}{c}_qa", (part.add_rest,), (part.start, 0, 3))
            transfers(f"{name}{c}_s1a", (part.up_term,))
            transfers(f"{name}{c}_s1b", (part.down_term,))
            transfers(f"{name}{c}_th", (part.third,))

    def attend_back(pair):
        qcols = pl.ds(pair * 128, 128)
        kcols = pl.ds(256 + pair * 128, 128)
        vcols = pl.ds(512 + pair * 128, 128)
        dk[...] = jnp.zeros_like(dk)
        dv[...] = jnp.zeros_like(dv)
        for i in range(8):
            at = pl.ds(i * 128, 128)
            deep = (i + 1) * 128
            do2 = dout[at, qcols]
            queries, grads = both(qp[at, qcols]), both(do2)
            prod = (do2.astype(F32) * ah[at, qcols].astype(F32)).T
            centre = jnp.concatenate(
                [jnp.sum(prod[h * HD : (h + 1) * HD], axis=0, keepdims=True) for h in range(2)], axis=1
            )
            probs = kept(pair, i)[...]
            ds = (probs.astype(F32) * (dot_nt(qp[:deep, vcols], grads) - centre)).astype(BF16)
            dq = own_parts(dot_nn(kt[qcols, :deep], ds)) * (HD**-0.5)
            dk[:deep, :] += dot_nn(ds, queries)
            dv[:deep, :] += dot_nn(probs, grads)
            qp[at, qcols] = turn(dq, at, -1.0).astype(BF16)
        for i in range(4):
            at = pl.ds(i * 256, 256)
            qp[at, kcols] = turn(dk[at, :] * LN2, at, -1.0).astype(BF16)
            qp[at, vcols] = dv[at, :].astype(BF16)

    transfers("attb0", (attend_back, 0))

    def pool_is_free():
        pl.semaphore_signal(free, inc=1, device_id=who["core"], device_id_type=MESH)

    transfers("attb1", (attend_back, 1), (pool_is_free,))
    for c in range(CHUNKS):
        transfers(f"p2.{c}", (spread_columns, qp, win, y, r2, c))
    transfers("pool", (pl.semaphore_wait, free, 1))

    def mix_rows(at, with_pair):
        branches = total(p1, f1, a1, at, with_pair)
        mixed[at, :] = (tokens[at, :].astype(F32) + branches + (bo[...] + b2[...])).astype(BF16)

    @step
    def mix():
        for c in range(CHUNKS):
            r1(c).arrived()
        each_row_block(mix_rows)
        send_out(0, *outputs[0])

    @step
    def bias():
        def part(i, carry):
            at = rows_at(i * 128, 128)
            sums = jnp.sum(qp[at, :].astype(F32), axis=0, keepdims=True)
            small[6:7, :] += sums[:, 0:1024]
            small[7:8, 0:QKV] += sums[:, 1024:IN_W]
            return carry

        small[...] = jnp.zeros_like(small)
        lax.fori_loop(0, 8, part, 0)

    def norm_of(at):
        values = tokens[at, :].astype(F32)
        center = values - jnp.mean(values, axis=-1, keepdims=True)
        rstd = lax.rsqrt(jnp.mean(center * center, axis=-1, keepdims=True) + 1e-05)
        return center * rstd, rstd

    def sums_of(at, with_pair):
        ngrad = total(y, f2, a2, at, with_pair)
        for n, term in enumerate((ngrad * norm_of(at)[0], ngrad, cot[at, :].astype(F32))):
            sums = jnp.sum(term, axis=0, keepdims=True)
            small[2 * n : 2 * n + 1, :] += sums[:, 0:1024]
            small[2 * n + 1 : 2 * n + 2, :] += sums[:, 1024:2048]

    def around(n, buffer, here, names, places):
        buffer[here] = small[...]
        copies = []
        for k, name in enumerate(names):
            i = n + k
            copies.append(remote(buffer.at[here], buffer.at[here], sms.at[i], smr.at[i], who[name]))
            copies[-1].start()

        def finish():
            for k, name in enumerate(names):
                there = buffer.at[places[k]]
                remote(there, there, sms.at[n + k], smr.at[n + k], who[name]).wait_recv()
            for c in copies:
                c.wait_send()

        return finish

    xi = xh * 2 + xl
    along_x = [((xi + way) % 4) * 2 for way in (3, 1, 2)]
    rounds = {}

    @step
    def sums():
        for c in range(CHUNKS):
            r2(c).arrived()
        each_row_block(sums_of)
        rounds["x"] = around(
            0,
            got_x,
            xi * 2 + core,
            ("core", "xp", "xm", "xx", "xp2", "xm2", "xx2"),
            [xi * 2 + 1 - core] + [p + core for p in along_x] + [p + 1 - core for p in along_x],
        )

    def back_norm(at, with_pair):
        xhat, rstd = norm_of(at)
        ex = total(y, f2, a2, at, with_pair) * gain[...]
        mean_e = jnp.mean(ex, axis=-1, keepdims=True)
        mean_ex = jnp.mean(ex * xhat, axis=-1, keepdims=True)
        tgrad[at, :] = (cot[at, :].astype(F32) + (ex - mean_e - xhat * mean_ex) * rstd).astype(BF16)

    transfers("back", (each_row_block, back_norm), (send_out, 1, *outputs[1]))

    @step
    def sum_x():
        rounds["x"]()
        small[0:6, :] = jnp.sum(got_x[:, 0:6, :], axis=0)
        small[6:8, :] = jnp.sum(got_x[pl.ds(4 * xh, 4), 6:8, :], axis=0)
        rounds["z"] = around(7, got.at[0], z, ("zp", "zm", "zz"), [(z + way) % 4 for way in (3, 1, 2)])

    @step
    def sum_z():
        rounds["z"]()
        small[...] = jnp.sum(got[0], axis=0)
        rounds["y"] = around(10, got.at[1], yy, ("yp", "ym", "yy"), [(yy + way) % 4 for way in (3, 1, 2)])

    @step
    def sum_y():
        rounds["y"]()
        small[0:6, :] = jnp.sum(got[1, :, 0:6, :], axis=0)

    @step
    def lasto():
        def rows(at):
            gout[at, :] = ro.total(at)

        ro.arrived()
        each(ROWS, rows)
        send_out(3, *outputs[3])

    @step
    def lastf():
        def rows(at):
            gin[at, QKV:IN_W] = rf.total(at)

        rf.arrived()
        each(ROWS, rows)

    @step
    def lastq():
        def rows(at):
            gin[at, 0:QKV] = rq.total(at)

        rq.arrived()
        each(ROWS, rows)

    for name in ORDER:
        steps[name]()
    send_out(2, *outputs[2])
    send_out(4, *outputs[4])

    for c in range(CHUNKS):
        r1(c).sent()
        r2(c).sent()
    for r in (ro, rf, rq):
        r.sent()
    for c in out_copies + fc_copies + qkv_copies:
        c.wait_send()
    for index, (src, dst) in enumerate(outputs):
        pltpu.make_async_copy(src, dst, out_of.at[index]).wait()


def block(*args):
    sems = pltpu.SemaphoreType.DMA

    def low(*shape):
        return pltpu.VMEM(shape, BF16)

    ring = [low(2, ROWS, D), low(2, 2, ROWS, D), low(KEEP, D), low(4, ROWS - KEEP, D)]
    rows_4d = low(4, 2, ROWS, D)
    smem = pl.BlockSpec(memory_space=pltpu.SMEM)
    return pl.pallas_call(
        block_kernel,
        out_shape=(
            jax.ShapeDtypeStruct((ROWS, D), BF16),
            jax.ShapeDtypeStruct((ROWS, D), BF16),
            jax.ShapeDtypeStruct((ROWS, IN_W), F32),
            jax.ShapeDtypeStruct((ROWS, OUT_W), F32),
            jax.ShapeDtypeStruct((8, 1024), F32),
        ),
        in_specs=[ANY, ANY, smem, ANY, VMEM, ANY, VMEM, ANY, VMEM, ANY] + [VMEM] * 5,
        out_specs=(ANY,) * 5,
        scratch_shapes=[
            low(ROWS, D), low(ROWS, D), low(256, ROWS), low(FC, ROWS),
            pltpu.VMEM((ROWS, IN_W), F32), pltpu.VMEM((ROWS, OUT_W), F32), pltpu.VMEM((8, 1024), F32),
            sems((9,)), sems((5,)),
            low(GROUP, D), rows_4d, low(D, IN_W), low(D, OUT_W),
            low(GROUP, OUT_W), low(GROUP, IN_W), low(GROUP, 256), low(2560, GROUP), rows_4d,
            pltpu.VMEM((GROUP, 128), F32), pltpu.VMEM((GROUP, 128), F32),
            pltpu.VMEM((GROUP, 128), F32), pltpu.VMEM((GROUP, 128), F32),
            *ring, *ring,
            low(2, ROWS, IN_W), low(2, 2, ROWS, IN_W), low(ROWS, IN_W),
            low(2, ROWS, OUT_W), low(2, 2, ROWS, OUT_W), low(ROWS, OUT_W),
            low(8 * ROWS, OUT_W),
            pltpu.VMEM((8, 8, 1024), F32), pltpu.VMEM((2, 4, 8, 1024), F32),
            low(256, GROUP), low(256, GROUP),
            sems((12,)), sems((12,)), sems((12,)), sems((12,)),
            sems((9,)), sems((9,)), sems((10,)), sems((10,)),
            sems((9,)), sems((9,)), sems((10,)), sems((10,)),
            sems((CHUNKS, 8)), sems((CHUNKS, 8)), sems((CHUNKS, 8)), sems((CHUNKS, 8)),
            sems((7,)), sems((7,)), sems((7,)), sems((7,)), sems((7,)), sems((7,)),
            sems((8,)), sems((8,)), sems((8,)), sems((8,)), sems((8,)), sems((8,)),
            sems((13,)), sems((13,)), pltpu.SemaphoreType.REGULAR,
        ],
        compiler_params=pltpu.CompilerParams(
            collective_id=0, has_side_effects=True, vmem_limit_bytes=VMEM_LIMIT
        ),
        name="block",
    )(*args)


def finish_kernel(
    mixed, tgrad, gin, gout, small,
    o_mixed, o_tgrad, gq, bq, go, bo, g1, b1, g2, b2, gain, shift,
    kept, sums, sem,
):
    def copy(index, src, dst):
        c = pltpu.make_async_copy(src, dst, sem.at[index])
        c.start()
        return c

    out, totals = copy(0, gout, kept), copy(1, small, sums)
    rest = [copy(2, mixed, o_mixed), copy(3, tgrad, o_tgrad), copy(4, gin.at[:, QKV:IN_W], g1)]
    for t in range(3):
        rest.append(copy(5 + t, gin.at[:, t * 256 : (t + 1) * 256], gq.at[t]))
    totals.wait()
    for t in range(3):
        bq[t : t + 1, :] = sums[6:7, t * 256 : (t + 1) * 256]
    b1[:, 0:256] = sums[6:7, QKV:1024]
    b1[:, 256:FC] = sums[7:8, 0:QKV]
    for n in range(2):
        cols = slice(n * 1024, (n + 1) * 1024)
        gain[:, cols] = sums[n : n + 1, :]
        shift[:, cols] = sums[2 + n : 3 + n, :]
        bo[:, cols] = sums[4 + n : 5 + n, :]
        b2[:, cols] = sums[4 + n : 5 + n, :]
    out.wait()
    go[...] = kept[:, 0:256].T
    for j in range(8):
        g2[j * 128 : (j + 1) * 128, :] = kept[:, 256 + j * 128 : 256 + (j + 1) * 128].T
    for c in rest:
        c.wait()


def finish(*args):
    def out(*shape):
        return jax.ShapeDtypeStruct(shape, F32)

    rows = jax.ShapeDtypeStruct((ROWS, D), BF16)
    shapes = (
        rows, rows, out(3, ROWS, 256), out(3, 256), out(256, ROWS), out(1, D), out(ROWS, FC), out(1, FC),
        out(FC, ROWS), out(1, D), out(1, D), out(1, D),
    )
    return pl.pallas_call(
        finish_kernel,
        out_shape=shapes,
        in_specs=[ANY] * 5,
        out_specs=(VMEM,) * 12,
        scratch_shapes=[
            pltpu.VMEM((ROWS, OUT_W), F32), pltpu.VMEM((8, 1024), F32), pltpu.SemaphoreType.DMA((8,))
        ],
        compiler_params=pltpu.CompilerParams(vmem_limit_bytes=VMEM_LIMIT),
        name="finish",
    )(*args)


def per_device(
    tokens, cotangent, seq_lengths, w_qkv, b_qkv, w_out, b_out, w_fc1, b_fc1, w_fc2, b_fc2, ln_gain, ln_bias
):
    lane = np.arange(128) % HD
    angle = np.float32(10000.0) ** (np.float32(-2.0) * (lane % (ROT // 2)).astype(np.float32) / np.float32(ROT))
    freq = jnp.asarray(np.where(lane < ROT, angle, 0.0).astype(np.float32))
    sign = jnp.asarray(np.where(lane < ROT // 2, -1.0, np.where(lane < ROT, 1.0, 0.0)).astype(np.float32))
    parts = block(
        tokens, cotangent, seq_lengths, jnp.transpose(w_qkv, (1, 0, 2)), b_qkv, w_out, b_out[None], w_fc1,
        b_fc1[None], w_fc2, b_fc2[None], ln_gain[None], ln_bias[None], freq[None], sign[None],
    )
    mixed, tgrad, gq, bq, go, bo, g1, b1, g2, b2, gain, shift = finish(*parts)
    return (
        mixed, tgrad, jnp.transpose(gq, (1, 0, 2)), bq, go, bo[0], g1, b1[0], g2, b2[0], gain[0], shift[0]
    )


def solution(mesh):
    in_specs = (
        P(("dp", "mp"), None),
        P(("dp", "mp"), None),
        P("dp", None),
        P("dp", None, "mp"),
        P(None, "mp"),
        P("mp", "dp"),
        P(),
        P("dp", "mp"),
        P("mp"),
        P("mp", "dp"),
        P(),
        P(),
        P(),
    )
    out_specs = (
        P(("dp", "mp"), None),
        P(("dp", "mp"), None),
        P("dp", None, "mp"),
        P(None, "mp"),
        P("mp", "dp"),
        P(),
        P("dp", "mp"),
        P("mp"),
        P("mp", "dp"),
        P(),
        P(),
        P(),
    )
    return jax.shard_map(
        per_device, mesh=mesh, in_specs=in_specs, out_specs=out_specs, check_vma=False
    )
```
